256 devices in a mesh: seq: 64 (over x, z, core), head: 4 (over y).
Axes of the slice: x: 4, y: 4, z: 8, core: 2. Of those that a mesh axis runs over, the one named last changes fastest.
Arguments:
- queries: bfloat16 [24576, 2048], P('seq', 'head'), may hold values from -120 to 120
- keys: bfloat16 [24576, 2048], P('seq', 'head'), may hold values from -5 to 5
- values: bfloat16 [24576, 2048], P('seq', 'head'), may hold values from -5 to 5
- directions: bfloat16 [24576, 2048], P('seq', 'head'), may hold values from -5 to 5
- beta_logit: float32 [16, 24576], P('head', 'seq'), may hold values from -3 to 7
- out_weight: bfloat16 [2048, 2048], P('head'), may hold values from -0.1875 to 0.1875
Outputs:
- mixed: bfloat16 [24576, 2048], P('seq', 'head')
The draws below stay inside these ranges and needn't reach their ends.
All inputs are finite; a program needn't handle non-finite values.
Results may differ from the reference program's by a relative error of at most 0.015.
Values may be sent and summed in bfloat16 or wider, within the bound.
A program may use at most 64 MiB of HBM per device.

```python
import math
import jax
import jax.numpy as jnp
from jax import lax

HEADS = 16
HEAD_DIM = 128
D = 2048
SUB = 128
WINDOW = 4
TOK_DEV = 384
TOKENS = 24576
N_SEQ = 64


def drawn_rows(key):
    width = HEADS * HEAD_DIM
    base_keys = jnp.clip(jax.random.normal(jax.random.fold_in(key, 11), (TOKENS, width), jnp.float32), -4.5, 4.5)
    base_queries = jnp.clip(jax.random.normal(jax.random.fold_in(key, 12), (TOKENS, width), jnp.float32), -4.5, 4.5)
    return (base_queries, base_keys)


def draw_queries(key, part):
    queries_out, keys_out = drawn_rows(key)
    return queries_out.astype(jnp.bfloat16)


def draw_keys(key, part):
    queries_out, keys_out = drawn_rows(key)
    return keys_out.astype(jnp.bfloat16)


def draw_beta_logit(key, part):
    shape_all = (HEADS, TOKENS)
    strong = jax.random.uniform(jax.random.fold_in(key, 21), shape_all, jnp.float32, 3.5, 7.0)
    softer = jax.random.uniform(jax.random.fold_in(key, 22), shape_all, jnp.float32, -3.0, 1.0)
    rarely = jax.random.bernoulli(jax.random.fold_in(key, 23), 1.0 / 64.0, shape_all)
    return jnp.where(rarely, softer, strong).astype(jnp.float32)


def with_spikes(drawn, key, source, target, shards_of, factor):
    owner, partner = [(jnp.arange(drawn.shape[axis_at]) // (drawn.shape[axis_at] // shards_of)).reshape([-1 if axis == axis_at else 1 for axis in range(drawn.ndim)]) for axis_at in (source, target)]
    chosen = jax.random.permutation(key, shards_of)[partner]
    strong = (owner == chosen) | (owner == (partner + shards_of // 2) % shards_of)
    return jnp.where(strong, factor * drawn, drawn)


def level_of(key, dims, pieces, smallest, top_value):
    level, own = 1.0, jax.random.fold_in(key, 6)
    for dim, blocks in pieces:
        steps = jnp.exp(jax.random.uniform(jax.random.fold_in(own, dim), (blocks,), jnp.float32, smallest / len(pieces), top_value / len(pieces)))
        level = level * jnp.repeat(steps, dims[dim] // blocks).reshape([-1 if axis == dim else 1 for axis in range(len(dims))])
    return level


def bell_draw(stream_key, extent, scale, bound, cuts=(), held_as=jnp.bfloat16):
    level = level_of(stream_key, extent, cuts, -0.22, 0.18) if cuts else 1.0
    drawn = jax.random.normal(stream_key, extent, jnp.float32) * scale * level
    return jnp.minimum(jnp.maximum(drawn, -bound), bound).astype(held_as)


def bell_draw_with(key, shape, scale, reach, pieces, heavy, held_as=jnp.bfloat16):
    values = scale * jax.random.normal(key, shape, jnp.float32)
    if pieces:
        values = values * level_of(key, shape, pieces, -0.22, 0.18)
    return jnp.clip(with_spikes(values, jax.random.fold_in(key, 3), *heavy), -reach, reach).astype(held_as)


def setup_inputs(seed: int = 0) -> dict:
    key_list = jax.random.split(jax.random.key(seed), 7)
    return {
        "queries": draw_queries(jax.random.fold_in(key_list[6], 71), 0),
        "keys": draw_keys(jax.random.fold_in(key_list[6], 71), 0),
        "values": bell_draw(key_list[2], (TOKENS, HEADS * HEAD_DIM), 1.0, 5.0, ((0, 64), (1, 4))),
        "directions": bell_draw(key_list[3], (TOKENS, HEADS * HEAD_DIM), 1.0, 5.0, ((0, 64), (1, 4))),
        "beta_logit": draw_beta_logit(jax.random.fold_in(key_list[6], 71), 0),
        "out_weight": bell_draw_with(key_list[5], (HEADS * HEAD_DIM, D), (HEADS * HEAD_DIM) ** -0.5, 0.1875, ((0, 4),), (0, 1, 4, 2.0)),
    }


highest = lax.Precision.HIGHEST

def product(pattern, first_op, second_op):
    return jnp.einsum(pattern, first_op, second_op, precision=highest)

def solve_unit(matrix):
    identity_run = jnp.eye(matrix.shape[0], dtype=matrix.dtype)
    return jax.scipy.linalg.solve_triangular(matrix, identity_run, lower=True, unit_diagonal=True)

def block_local(query_rows, key_rows, direction_rows, logits, run_size):
    head_count, length, head_size = query_rows.shape
    run_count = length // run_size
    shape_runs = (head_count, run_count, run_size, head_size)
    queries32 = query_rows.astype(jnp.float32).reshape(shape_runs)
    keys32 = key_rows.astype(jnp.float32).reshape(shape_runs)
    raw_dirs = direction_rows.astype(jnp.float32)
    unit_dirs = (raw_dirs * lax.rsqrt(lax.optimization_barrier(jnp.sum(raw_dirs * raw_dirs, axis=-1, keepdims=True)) + 1e-06)).reshape(shape_runs)
    betas = (2.0 * jax.nn.sigmoid(logits.astype(jnp.float32))).reshape(head_count, run_count, run_size)
    ones_run = jnp.ones((run_size, run_size), jnp.float32)
    strict_lower = jnp.tril(ones_run, -1)
    inclusive = jnp.tril(ones_run, 0)
    strict_upper = jnp.triu(ones_run, 1)
    identity_run = jnp.eye(run_size, dtype=jnp.float32)
    grams = product('hnce,hnde->hncd', unit_dirs, unit_dirs)
    system = identity_run + grams * strict_lower * betas[:, :, None, :]
    inverse = jax.vmap(solve_unit)(system.reshape(-1, run_size, run_size)).reshape(system.shape)
    coeffs = betas[:, :, :, None] * inverse
    coeff_dirs = product('hnac,hncd->hnad', coeffs, unit_dirs)
    coeff_back = product('hnca,hncd->hnad', coeffs, unit_dirs)
    identity_head = jnp.eye(head_size, dtype=jnp.float32)
    run_maps = identity_head - product('hncd,hnce->hnde', unit_dirs, coeff_dirs)
    query_dirs = product('hnid,hnad->hnia', queries32, unit_dirs) * inclusive
    query_start = queries32 - product('hnia,hnad->hnid', query_dirs, coeff_dirs)
    key_dirs = product('hnjd,hncd->hnjc', keys32, unit_dirs) * strict_upper
    key_end = keys32 - product('hnjc,hncd->hnjd', key_dirs, coeff_back)
    mixed_dirs = product('hnac,hnjc->hnaj', coeffs, key_dirs)
    inside = product('hnid,hnjd->hnij', queries32, keys32) - product('hnia,hnaj->hnij', query_dirs, mixed_dirs)
    inside = jnp.where(inclusive > 0, inside, -jnp.inf)
    carried = jnp.zeros((head_count, length, head_size), jnp.float32)
    prefix = jnp.broadcast_to(identity_head, (head_count, head_size, head_size))
    row_parts = []
    query_parts = []
    for index_run in range(run_count):
        starts = query_start[:, index_run]
        query_parts.append(product('hid,hde->hie', starts, prefix))
        across = product('hid,hjd->hij', starts, carried)
        before = index_run * run_size
        after = length - before - run_size
        filler = jnp.full((head_count, run_size, after), -jnp.inf, jnp.float32)
        row_parts.append(jnp.concatenate([across[:, :, :before], inside[:, index_run], filler], axis=2))
        carried = product('hjd,hed->hje', carried, run_maps[:, index_run])
        carried = lax.dynamic_update_slice_in_dim(carried, key_end[:, index_run], before, 1)
        prefix = product('hde,hef->hdf', run_maps[:, index_run], prefix)
    own_scores = jnp.concatenate(row_parts, axis=1)
    query_block = jnp.concatenate(query_parts, axis=1)
    return (own_scores, query_block, carried, prefix)

def attend(score_parts, value_parts, head_size):
    scores = jnp.concatenate(score_parts, axis=2) * (1.0 / math.sqrt(head_size))
    maxima = lax.optimization_barrier(jnp.max(scores, axis=2, keepdims=True))
    weights = jnp.exp(scores - maxima)
    totals = lax.optimization_barrier(jnp.sum(weights, axis=2, keepdims=True))
    rounded = weights.astype(jnp.bfloat16)
    values_all = jnp.concatenate(value_parts, axis=1)
    attended = jnp.einsum('hik,hkd->hid', rounded.astype(jnp.float32), values_all.astype(jnp.float32), precision=highest)
    return (attended / totals).astype(jnp.bfloat16)

def reference(queries, keys, values, directions, beta_logit, out_weight):

    def blocks(array):
        return array.reshape(N_SEQ, TOK_DEV, HEADS, HEAD_DIM).transpose(0, 2, 1, 3)
    query_all = blocks(queries)
    key_all = blocks(keys)
    value_all = blocks(values)
    dir_all = blocks(directions)
    logit_all = beta_logit.reshape(HEADS, N_SEQ, TOK_DEV).transpose(1, 0, 2)

    def pick(array, index_block):
        return lax.dynamic_index_in_dim(array, index_block, 0, keepdims=False)

    def local_pass(index_block):
        result = block_local(pick(query_all, index_block), pick(key_all, index_block), pick(dir_all, index_block), pick(logit_all, index_block), SUB)
        return (result[1], result[2], result[3])
    block_ids = jnp.arange(N_SEQ, dtype=jnp.int32)
    query_tilde, key_tilde, block_maps = lax.map(local_pass, block_ids)
    key_rounded = key_tilde.astype(jnp.bfloat16)
    identity_head = jnp.eye(HEAD_DIM, dtype=jnp.float32)

    def window_pass(index_block):
        own_scores, query_block, unused_keys, unused_map = block_local(pick(query_all, index_block), pick(key_all, index_block), pick(dir_all, index_block), pick(logit_all, index_block), SUB)
        score_parts = [own_scores]
        value_parts = [pick(value_all, index_block)]
        composed = jnp.broadcast_to(identity_head, (HEADS, HEAD_DIM, HEAD_DIM))
        for distance in range(1, WINDOW + 1):
            source = jnp.maximum(index_block - distance, 0).astype(jnp.int32)
            if distance > 1:
                middle = jnp.maximum(index_block - distance + 1, 0).astype(jnp.int32)
                composed = product('hde,hef->hdf', composed, pick(block_maps, middle))
            moved = product('hjd,hed->hje', pick(key_rounded, source).astype(jnp.float32), composed)
            remote = product('hid,hjd->hij', query_block, moved)
            score_parts.append(jnp.where(index_block >= distance, remote, -jnp.inf))
            value_parts.append(pick(value_all, source))
        return attend(score_parts, value_parts, HEAD_DIM)
    outputs = lax.map(window_pass, block_ids)
    attn = outputs.transpose(0, 2, 1, 3).reshape(TOKENS, HEADS * HEAD_DIM)
    return jnp.dot(attn.astype(jnp.float32), out_weight.astype(jnp.float32), preferred_element_type=jnp.float32).astype(jnp.bfloat16)
```

```python
import functools
import math

import jax
import jax.numpy as jnp
from jax import lax
from jax.experimental import pallas as pl
from jax.experimental.pallas import tpu as pltpu
from jax.sharding import PartitionSpec as P

F32, BF16 = jnp.float32, jnp.bfloat16
MESH = pl.DeviceIdType.MESH
SUB = 128
SCALE = math.log2(math.e) / math.sqrt(128.0)
ABSENT = -1e30
GROUP = 2

NN = (((1,), (0,)), ((), ()))
NT = (((1,), (1,)), ((), ()))
TN = (((0,), (0,)), ((), ()))


def dot1(a, b, dims=NN):
    return lax.dot_general(a, b, dims, preferred_element_type=F32)


def halves(x):
    high = x.astype(BF16)
    return high, (x - high.astype(F32)).astype(BF16)


def dot3(a, b, dims=NN):
    ah, al = halves(a)
    bh, bl = halves(b)
    k = dims[0][1][0]
    both = jnp.concatenate([bh, bl], 1 - k)
    r = dot1(jnp.concatenate([ah, al], 1), jnp.concatenate([both, both], k), dims)
    half = r.shape[1] // 2
    return r[:, :half] + r[:, half:]


def twice(a, b, dims=NN):
    k = dims[0][1][0]
    return dot1(jnp.concatenate(halves(a), 1), jnp.concatenate([b, b], k), dims)


def each(f, *lists):
    return [f(*t) for t in zip(*lists)]


def grid_ids():
    return (
        lax.broadcasted_iota(jnp.int32, (SUB, SUB), 0),
        lax.broadcasted_iota(jnp.int32, (SUB, SUB), 1),
    )


def local_heads(q, k, w, beta):
    runs = q[0].shape[0] // SUB
    row, col = grid_ids()
    eye = row == col

    def cut(x):
        return [a[r * SUB : (r + 1) * SUB] for a in x for r in range(runs)]

    qr, kr, wr = cut(q), cut(k), cut(w)
    br = [b[:, r * SUB : (r + 1) * SUB] for b in beta for r in range(runs)]
    t = each(lambda a, b, c: dot1(jnp.concatenate([c, a, b], 0), c, NT), qr, kr, wr)
    g = [x[:SUB] for x in t]
    a = [jnp.where(row >= col, x[SUB : 2 * SUB], 0.0) for x in t]
    c = [jnp.where(row < col, x[2 * SUB :], 0.0) for x in t]
    d_row = each(lambda x, b: b / (jnp.sum(jnp.where(eye, x, 0.0), 0, keepdims=True) + 1e-6), g, br)
    d_col = [jnp.sum(jnp.where(eye, x, 0.0), 1, keepdims=True) for x in d_row]

    def corner(b):
        return ((row // (2 * b)) == (col // (2 * b))) & ((row & b) != 0) & ((col & b) == 0)

    first = corner(1)
    inv = each(
        lambda x, dr, dc: jnp.where(eye, dr, jnp.where(first, -(x * dc) * dr, 0.0)), g, d_row, d_col
    )
    for b in (2, 4, 8, 16, 32, 64):
        mask = corner(b)
        m = [jnp.where(mask, x, 0.0) for x in g]
        z = each(lambda x, y: dot3(x, y), inv, m)
        inv = each(lambda x, y: x - dot3(y, x), inv, z)
    f = each(lambda x, y: dot3(x, y, NT), c, inv)
    ke = each(lambda x, y, d: x.astype(F32) - twice(y, d), kr, f, wr)
    y = each(lambda x, d: twice(x, d), inv, wr)
    unit = eye.astype(F32)

    def run_map(d, x):
        return unit - dot1(jnp.concatenate([d, d], 0), jnp.concatenate(halves(x), 0), TN)

    p = each(run_map, wr, y)
    qs = each(lambda x, e, z: (x.astype(F32) - dot3(e, z)) * SCALE, qr, a, y)
    ins = each(lambda x, z, e, h: (dot1(x, z, NT) - dot3(e, h, NT)) * SCALE, qr, kr, a, f)
    ins = [jnp.where(row >= col, x, -jnp.inf) for x in ins]
    out = []
    for i in range(len(q)):
        e1, e2, e3 = ke[3 * i : 3 * i + 3]
        p1, p2, p3 = p[3 * i : 3 * i + 3]
        q1, q2, q3 = qs[3 * i : 3 * i + 3]
        c2 = jnp.concatenate([dot3(e1, p2, NT), e2], 0)
        kt = jnp.concatenate([dot3(c2, p3, NT), e3], 0).astype(BF16)
        prefix = dot3(p2, p1)
        qt = jnp.concatenate([q1, dot3(q2, p1), dot3(q3, prefix)], 0)
        s2 = jnp.concatenate([dot3(q2, e1, NT), ins[3 * i + 1]], 1)
        s3 = jnp.concatenate([dot3(q3, c2, NT), ins[3 * i + 2]], 1)
        out.append((kt, qt, dot3(p3, prefix), [ins[3 * i], s2, s3]))
    return out


def wide(x, count=1):
    x = jnp.broadcast_to(x, (SUB, SUB))
    return x if count == 1 else jnp.concatenate([x] * count, 1)


def kernel(
    q, k, v, w, beta, wt, out,
    kbuf, kmid, qbuf, qmid, vbuf, pbuf, qn, oacc, mst, lst, osend, ofar, lsend, lfar, abuf, wbuf, wrel,
    send, recv, own,
):
    n_seq, n_head = lax.axis_size("seq"), lax.axis_size("head")
    s, h = lax.axis_index("seq"), lax.axis_index("head")
    nxt, prv = lax.rem(s + 1, n_seq), lax.rem(s + n_seq - 1, n_seq)
    nxt2, prv2 = lax.rem(s + 2, n_seq), lax.rem(s + n_seq - 2, n_seq)
    up, down, across = lax.rem(h + 1, n_head), lax.rem(h + n_head - 1, n_head), lax.rem(h + 2, n_head)
    length = q.shape[0]
    runs = length // SUB
    heads = q.shape[1] // SUB
    groups = heads // GROUP
    width = out.shape[1]
    half = length // 2
    depth_half = wt.shape[0] // 2
    row, col = grid_ids()
    eye = row == col

    barrier = pltpu.get_barrier_semaphore()
    for device in ({"seq": prv}, {"seq": nxt}, {"seq": prv2}, {"head": up}, {"head": down}):
        pl.semaphore_signal(barrier, inc=1, device_id=device, device_id_type=MESH)
    pl.semaphore_wait(barrier, 5)

    def remote(src, dst, i, device):
        return pltpu.make_async_remote_copy(
            src_ref=src, dst_ref=dst, send_sem=send.at[i], recv_sem=recv.at[i],
            device_id=device, device_id_type=MESH,
        )

    def heads_of(g):
        return pl.ds(g * GROUP, GROUP)

    def columns(c):
        return pl.ds(pl.multiple_of(c * width, width), width)

    lo, hi = pl.ds(0, depth_half), pl.ds(depth_half, depth_half)
    v_first = remote(v, vbuf.at[0], 0, {"seq": nxt})
    v_second = remote(vbuf.at[0], vbuf.at[1], 1, {"seq": nxt})
    w_up = remote(wt.at[:, columns(up)], wbuf.at[0], 2, {"head": up})
    w_down = remote(wt.at[:, columns(down)], wbuf.at[1], 3, {"head": down})
    w_rel_up = remote(wt.at[lo, columns(across)], wrel.at[0], 4, {"head": up})
    w_rel_down = remote(wt.at[hi, columns(across)], wrel.at[1], 5, {"head": down})
    w_far_up = remote(wrel.at[0], wbuf.at[2, lo], 6, {"head": up})
    w_far_down = remote(wrel.at[1], wbuf.at[2, hi], 7, {"head": down})

    def k_first(g):
        return remote(kbuf.at[0, heads_of(g)], kbuf.at[1, heads_of(g)], 8 + g, {"seq": nxt})

    def k_second(g):
        return remote(kmid.at[heads_of(g)], kbuf.at[2, heads_of(g)], 10 + g, {"seq": nxt})

    def q_first(g):
        return remote(qbuf.at[0, heads_of(g)], qbuf.at[1, heads_of(g)], 12 + g, {"seq": prv})

    def q_second(g):
        return remote(qmid.at[heads_of(g)], qbuf.at[2, heads_of(g)], 14 + g, {"seq": prv})

    def o_back(g):
        return remote(osend.at[heads_of(g)], ofar.at[heads_of(g)], 16 + g, {"seq": nxt2})

    def l_back(g):
        return remote(lsend.at[heads_of(g)], lfar.at[heads_of(g)], 18 + g, {"seq": nxt2})

    def a_up(g):
        return remote(abuf.at[0, heads_of(g)], abuf.at[1, heads_of(g)], 20 + g, {"head": up})

    def a_down(g):
        return remote(abuf.at[0, heads_of(g)], abuf.at[2, heads_of(g)], 22 + g, {"head": down})

    def a_far_up(g):
        part = pl.ds(0, half)
        return remote(abuf.at[1, heads_of(g), part], abuf.at[3, heads_of(g), part], 24 + g, {"head": up})

    def a_far_down(g):
        part = pl.ds(half, half)
        return remote(abuf.at[2, heads_of(g), part], abuf.at[3, heads_of(g), part], 26 + g, {"head": down})

    v_first.start()
    w_rel_up.start()
    w_rel_down.start()
    w_up.start()
    w_down.start()
    w_own = pltpu.make_async_copy(wt.at[:, columns(h)], wbuf.at[3], own)
    w_own.start()

    lanes = [pl.ds(x * SUB, SUB) for x in range(heads)]
    done = local_heads(
        [q[:, x] for x in lanes],
        [k[:, x] for x in lanes],
        [w[:, x] for x in lanes],
        [2.0 * jax.nn.sigmoid(beta[x : x + 1, :]) for x in range(heads)],
    )
    for x, (kt, qt, pb, _) in enumerate(done):
        kbuf[0, x] = kt
        qh, ql = halves(qt)
        qbuf[0, x] = qh
        qn[x, :, :SUB] = qh
        qn[x, :, SUB:] = ql
        ph, plow = halves(pb)
        pbuf[x, :, :SUB] = ph
        pbuf[x, :, SUB:] = plow
        if x % GROUP == GROUP - 1:
            k_first(x // GROUP).start()
            q_first(x // GROUP).start()
    v_first.wait_recv()
    v_second.start()
    w_rel_up.wait_recv()
    w_far_up.start()
    w_rel_down.wait_recv()
    w_far_down.start()

    for x, (_, _, _, scores) in enumerate(done):
        for r, sc in enumerate(scores):
            rows = pl.ds(r * SUB, SUB)
            top = jnp.max(sc, 1, keepdims=True)
            e = jnp.exp2(sc - top)
            mst[x, rows] = wide(top)
            lst[x, rows] = wide(jnp.sum(e, 1, keepdims=True))
            oacc[x, rows] = dot1(e.astype(BF16), v[: (r + 1) * SUB, lanes[x]])

    @pl.loop(0, groups)
    def _(g):
        k_first(g).wait_recv()
        for i in range(GROUP):
            x = g * GROUP + i
            kk = kbuf[1, x]
            kmid[x] = dot1(jnp.concatenate([kk, kk], 1), pbuf[x], NT).astype(BF16)
        k_second(g).start()
        q_first(g).wait_recv()
        for i in range(GROUP):
            x = g * GROUP + i
            qq = qbuf[1, x]
            pp = jnp.concatenate([pbuf[x, :, :SUB], pbuf[x, :, SUB:]], 0)
            qmid[x] = dot1(jnp.concatenate([qq, qq], 1), pp).astype(BF16)
        q_second(g).start()

    near = jnp.where(s >= 1, 0.0, ABSENT).astype(F32)
    beyond = jnp.where(s >= 2, 0.0, ABSENT).astype(F32)

    def window_scores(queries, keys):
        sc = dot1(queries, keys, NT)
        return jnp.concatenate([sc[:, :length] + near, sc[:, length:] + beyond], 1)

    def window_arrays(x):
        keys = jnp.concatenate([kbuf[1, x], kbuf[2, x]], 0)
        lane = pl.ds(pl.multiple_of(x * SUB, SUB), SUB)
        return jnp.concatenate([keys, keys], 1), jnp.concatenate([vbuf[0, :, lane], vbuf[1, :, lane]], 0)

    v_second.wait_recv()

    @pl.loop(0, groups)
    def _(g):
        k_second(g).wait_recv()
        q_second(g).wait_recv()
        for i in range(GROUP):
            x = g * GROUP + i
            qq = qbuf[2, x]
            pp = jnp.concatenate([pbuf[x, :, :SUB], pbuf[x, :, SUB:]], 0)
            moved = jnp.concatenate(halves(dot1(jnp.concatenate([qq, qq], 1), pp)), 1)
            keys, vals = window_arrays(x)
            for r in range(runs):
                rows = pl.ds(r * SUB, SUB)
                sc = window_scores(moved[r * SUB : (r + 1) * SUB], keys)
                top = jnp.max(sc, 1, keepdims=True)
                e = jnp.exp2(sc - top)
                total = jnp.sum(e, 1, keepdims=True)
                osend[x, rows] = (dot1(e.astype(BF16), vals) / total).astype(BF16)
                level = wide(top + jnp.log2(total))
                lsend[x, r : r + 1] = jnp.sum(jnp.where(eye, level, 0.0), 0, keepdims=True)
        o_back(g).start()
        l_back(g).start()

    @pl.loop(0, groups)
    def _(g):
        for i in range(GROUP):
            x = g * GROUP + i
            keys, vals = window_arrays(x)
            for r in range(runs):
                rows = pl.ds(r * SUB, SUB)
                sc = window_scores(qn[x, rows], keys)
                before = mst[x, rows]
                top = jnp.maximum(before, wide(jnp.max(sc, 1, keepdims=True)))
                e = jnp.exp2(sc - jnp.concatenate([top] * (2 * runs), 1))
                keep = jnp.exp2(before - top)
                mst[x, rows] = top
                lst[x, rows] = lst[x, rows] * keep + wide(jnp.sum(e, 1, keepdims=True))
                oacc[x, rows] = oacc[x, rows] * keep + dot1(e.astype(BF16), vals)

    @pl.loop(0, groups)
    def _(g):
        o_back(g).wait_recv()
        l_back(g).wait_recv()
        for i in range(GROUP):
            x = g * GROUP + i
            for r in range(runs):
                rows = pl.ds(r * SUB, SUB)
                level = jnp.where(s >= 3, lfar[x, r : r + 1], ABSENT)
                level = wide(jnp.sum(jnp.where(eye, level, 0.0), 1, keepdims=True))
                before = mst[x, rows]
                top = jnp.maximum(before, level)
                keep, other = jnp.exp2(before - top), jnp.exp2(level - top)
                total = lst[x, rows] * keep + other
                mix = oacc[x, rows] * keep + ofar[x, rows].astype(F32) * other
                abuf[0, x, rows] = (mix / total).astype(BF16)
        a_up(g).start()
        a_down(g).start()

    w_up.wait_recv()
    w_down.wait_recv()
    w_far_up.wait_recv()
    w_far_down.wait_recv()

    def project(slot, weight):
        joined = jnp.concatenate([abuf[slot, x] for x in range(heads)], 1)
        return dot1(joined, weight)

    @pl.loop(0, groups)
    def _(g):
        a_up(g).wait_recv()
        a_far_up(g).start()
        a_down(g).wait_recv()
        a_far_down(g).start()

    w_own.wait()
    total = project(1, wbuf[0]) + project(2, wbuf[1]) + project(0, wbuf[3])
    for g in range(groups):
        a_far_up(g).wait_recv()
        a_far_down(g).wait_recv()
    out[...] = (total + project(3, wbuf[2])).astype(BF16)
    for copy in (v_first, v_second, w_up, w_down, w_rel_up, w_rel_down, w_far_up, w_far_down):
        copy.wait_send()

    @pl.loop(0, groups)
    def _(g):
        for copy in (k_first, k_second, q_first, q_second, o_back, l_back, a_up, a_down, a_far_up, a_far_down):
            copy(g).wait_send()


def per_device(q, k, v, w, beta, wt):
    length, width = q.shape
    heads = width // SUB
    stat = pltpu.VMEM((heads, length, SUB), F32)
    rows = pltpu.VMEM((heads, length, SUB), BF16)

    def rows_of(count):
        return pltpu.VMEM((count, heads, length, SUB), BF16)

    scratch = [
        rows_of(3), rows, rows_of(3), rows,
        pltpu.VMEM((2, length, width), BF16),
        pltpu.VMEM((heads, SUB, 2 * SUB), BF16),
        pltpu.VMEM((heads, length, 2 * SUB), BF16),
        stat, stat, stat, rows, rows,
        pltpu.VMEM((heads, 8, SUB), F32),
        pltpu.VMEM((heads, 8, SUB), F32),
        rows_of(4),
        pltpu.VMEM((4, width, width), BF16),
        pltpu.VMEM((2, width // 2, width), BF16),
        pltpu.SemaphoreType.DMA((28,)),
        pltpu.SemaphoreType.DMA((28,)),
        pltpu.SemaphoreType.DMA,
    ]
    vmem = pl.BlockSpec(memory_space=pltpu.VMEM)
    return pl.pallas_call(
        kernel,
        out_shape=jax.ShapeDtypeStruct((length, width), BF16),
        in_specs=[vmem] * 5 + [pl.BlockSpec(memory_space=pl.ANY)],
        out_specs=vmem,
        scratch_shapes=scratch,
        compiler_params=pltpu.CompilerParams(
            collective_id=0, has_side_effects=True, vmem_limit_bytes=56 << 20
        ),
    )(q, k, v, w, beta, wt)


def solution(mesh):
    return jax.shard_map(
        per_device,
        mesh=mesh,
        in_specs=(P("seq", "head"),) * 4 + (P("head", "seq"), P("head", None)),
        out_specs=P("seq", "head"),
        check_vma=False,
    )
```

```python
import functools
import math

import jax
import jax.numpy as jnp
from jax import lax
from jax.experimental import pallas as pl
from jax.experimental.pallas import tpu as pltpu
from jax.sharding import PartitionSpec as P

F32, BF16 = jnp.float32, jnp.bfloat16
MESH = pl.DeviceIdType.MESH
SUB = 128
SCALE = math.log2(math.e) / math.sqrt(128.0)
ABSENT = -1e30
GROUP = 1
BATCH = 2

NN = (((1,), (0,)), ((), ()))
NT = (((1,), (1,)), ((), ()))
TN = (((0,), (0,)), ((), ()))


def dot1(a, b, dims=NN):
    return lax.dot_general(a, b, dims, preferred_element_type=F32)


def halves(x):
    high = x.astype(BF16)
    return high, (x - high.astype(F32)).astype(BF16)


def dot3(a, b, dims=NN):
    ah, al = halves(a)
    bh, bl = halves(b)
    k = dims[0][1][0]
    both = jnp.concatenate([bh, bl], 1 - k)
    r = dot1(jnp.concatenate([ah, al], 1), jnp.concatenate([both, both], k), dims)
    half = r.shape[1] // 2
    return r[:, :half] + r[:, half:]


def twice(a, b, dims=NN):
    k = dims[0][1][0]
    return dot1(jnp.concatenate(halves(a), 1), jnp.concatenate([b, b], k), dims)


def each(f, *lists):
    return [f(*t) for t in zip(*lists)]


def grid_ids():
    return (
        lax.broadcasted_iota(jnp.int32, (SUB, SUB), 0),
        lax.broadcasted_iota(jnp.int32, (SUB, SUB), 1),
    )


def local_heads(q, k, w, beta):
    runs = q[0].shape[0] // SUB
    row, col = grid_ids()
    eye = row == col

    def cut(x):
        return [a[r * SUB : (r + 1) * SUB] for a in x for r in range(runs)]

    qr, kr, wr = cut(q), cut(k), cut(w)
    br = [b[:, r * SUB : (r + 1) * SUB] for b in beta for r in range(runs)]
    t = each(lambda a, b, c: dot1(jnp.concatenate([c, a, b], 0), c, NT), qr, kr, wr)
    g = [x[:SUB] for x in t]
    a = [jnp.where(row >= col, x[SUB : 2 * SUB], 0.0) for x in t]
    c = [jnp.where(row < col, x[2 * SUB :], 0.0) for x in t]
    d_row = each(lambda x, b: b / (jnp.sum(jnp.where(eye, x, 0.0), 0, keepdims=True) + 1e-6), g, br)
    d_col = [jnp.sum(jnp.where(eye, x, 0.0), 1, keepdims=True) for x in d_row]

    def corner(b):
        return ((row // (2 * b)) == (col // (2 * b))) & ((row & b) != 0) & ((col & b) == 0)

    first = corner(1)
    inv = each(
        lambda x, dr, dc: jnp.where(eye, dr, jnp.where(first, -(x * dc) * dr, 0.0)), g, d_row, d_col
    )
    for b in (2, 4, 8, 16, 32, 64):
        mask = corner(b)
        m = [jnp.where(mask, x, 0.0) for x in g]
        z = each(lambda x, y: dot3(x, y), inv, m)
        inv = each(lambda x, y: x - dot3(y, x), inv, z)
    f = each(lambda x, y: dot3(x, y, NT), c, inv)
    ke = each(lambda x, y, d: x.astype(F32) - twice(y, d), kr, f, wr)
    y = each(lambda x, d: twice(x, d), inv, wr)
    unit = eye.astype(F32)

    def run_map(d, x):
        return unit - dot1(jnp.concatenate([d, d], 0), jnp.concatenate(halves(x), 0), TN)

    p = each(run_map, wr, y)
    qs = each(lambda x, e, z: (x.astype(F32) - dot3(e, z)) * SCALE, qr, a, y)
    ins = each(lambda x, z, e, h: (dot1(x, z, NT) - dot3(e, h, NT)) * SCALE, qr, kr, a, f)
    ins = [jnp.where(row >= col, x, -jnp.inf) for x in ins]
    out = []
    for i in range(len(q)):
        e1, e2, e3 = ke[3 * i : 3 * i + 3]
        p1, p2, p3 = p[3 * i : 3 * i + 3]
        q1, q2, q3 = qs[3 * i : 3 * i + 3]
        c2 = jnp.concatenate([dot3(e1, p2, NT), e2], 0)
        kt = jnp.concatenate([dot3(c2, p3, NT), e3], 0).astype(BF16)
        prefix = dot3(p2, p1)
        qt = jnp.concatenate([q1, dot3(q2, p1), dot3(q3, prefix)], 0)
        s2 = jnp.concatenate([dot3(q2, e1, NT), ins[3 * i + 1]], 1)
        s3 = jnp.concatenate([dot3(q3, c2, NT), ins[3 * i + 2]], 1)
        out.append((kt, qt, dot3(p3, prefix), [ins[3 * i], s2, s3]))
    return out


def wide(x, count=1):
    x = jnp.broadcast_to(x, (SUB, SUB))
    return x if count == 1 else jnp.concatenate([x] * count, 1)


def kernel(
    q_in, k_in, v_in, w_in, beta, wt, out,
    q, k, v, w, kbuf, kmid, qbuf, qmid, vbuf, pbuf, qn, oacc, mst, lst, osend, ofar, lsend, lfar, abuf, wbuf, wrel,
    acc, send, recv, own,
):
    n_seq, n_head = lax.axis_size("seq"), lax.axis_size("head")
    s, h = lax.axis_index("seq"), lax.axis_index("head")
    nxt, prv = lax.rem(s + 1, n_seq), lax.rem(s + n_seq - 1, n_seq)
    nxt2, prv2 = lax.rem(s + 2, n_seq), lax.rem(s + n_seq - 2, n_seq)
    up, down, across = lax.rem(h + 1, n_head), lax.rem(h + n_head - 1, n_head), lax.rem(h + 2, n_head)
    even = lax.rem(s, 2) == 0
    length = q.shape[0]
    runs = length // SUB
    heads = q.shape[1] // SUB
    groups = heads // GROUP
    width = out.shape[1]
    half = length // 2
    depth_half = wt.shape[0] // 2
    row, col = grid_ids()
    eye = row == col
    lanes = [pl.ds(x * SUB, SUB) for x in range(heads)]

    loads = [
        pltpu.make_async_copy(src, dst, own.at[i])
        for i, (src, dst) in enumerate(((w_in, w), (k_in, k), (q_in, q), (v_in, v)))
    ]
    for copy in loads:
        copy.start()

    barrier = pltpu.get_barrier_semaphore()
    for device in ({"seq": prv}, {"seq": nxt}, {"seq": prv2}, {"head": up}, {"head": down}):
        pl.semaphore_signal(barrier, inc=1, device_id=device, device_id_type=MESH)
    pl.semaphore_wait(barrier, 5)

    def remote(src, dst, i, device, sent=None):
        return pltpu.make_async_remote_copy(
            src_ref=src, dst_ref=dst, send_sem=send.at[i if sent is None else sent], recv_sem=recv.at[i],
            device_id=device, device_id_type=MESH,
        )

    def heads_of(g):
        return pl.ds(g * GROUP, GROUP)

    def columns(c):
        return pl.ds(pl.multiple_of(c * width, width), width)

    core = lax.rem(s, 2)
    twin = s + 1 - 2 * core
    part = depth_half // 2

    def rows_at(start, size):
        return pl.ds(pl.multiple_of(start, part), size)

    mine = rows_at(core * depth_half, depth_half)
    lo, hi = rows_at(core * depth_half, part), rows_at(core * depth_half + part, part)
    v_first = remote(v_in, vbuf.at[0], 0, {"seq": nxt})
    v_direct = remote(v_in, vbuf.at[1], 1, {"seq": nxt2}, 8 + 10 * groups)
    v_passed = remote(vbuf.at[0], vbuf.at[1], 1, {"seq": nxt})
    w_up = remote(wt.at[mine, columns(up)], wbuf.at[0, mine], 2, {"head": up})
    w_down = remote(wt.at[mine, columns(down)], wbuf.at[1, mine], 3, {"head": down})
    w_rel_up = remote(wt.at[lo, columns(across)], wrel.at[0], 4, {"head": up})
    w_rel_down = remote(wt.at[hi, columns(across)], wrel.at[1], 5, {"head": down})
    w_far_up = remote(wrel.at[0], wbuf.at[2, lo], 6, {"head": up})
    w_far_down = remote(wrel.at[1], wbuf.at[2, hi], 7, {"head": down})
    w_twin = [
        remote(wbuf.at[i, mine], wbuf.at[i, mine], 9 + 10 * groups + i, {"seq": twin}) for i in range(3)
    ]
    w_own = pltpu.make_async_copy(wt.at[:, columns(h)], wbuf.at[3], own.at[4])

    def k_first(g):
        return remote(kbuf.at[0, heads_of(g)], kbuf.at[1, heads_of(g)], 8 + g, {"seq": nxt})

    def k_second(g):
        return remote(kmid.at[heads_of(g)], kbuf.at[2, heads_of(g)], 8 + groups + g, {"seq": nxt})

    def q_first(g):
        return remote(qbuf.at[0, heads_of(g)], qbuf.at[1, heads_of(g)], 8 + 2 * groups + g, {"seq": prv})

    def q_second(g):
        return remote(qmid.at[heads_of(g)], qbuf.at[2, heads_of(g)], 8 + 3 * groups + g, {"seq": prv})

    def o_back(g):
        return remote(osend.at[heads_of(g)], ofar.at[heads_of(g)], 8 + 4 * groups + g, {"seq": nxt2})

    def l_back(g):
        return remote(lsend.at[heads_of(g)], lfar.at[heads_of(g)], 8 + 5 * groups + g, {"seq": nxt2})

    def a_up(g):
        return remote(abuf.at[0, heads_of(g)], abuf.at[1, heads_of(g)], 8 + 6 * groups + g, {"head": up})

    def a_down(g):
        return remote(abuf.at[0, heads_of(g)], abuf.at[2, heads_of(g)], 8 + 7 * groups + g, {"head": down})

    def a_far_up(g):
        part = pl.ds(0, half)
        return remote(
            abuf.at[1, heads_of(g), part], abuf.at[3, heads_of(g), part], 8 + 8 * groups + g, {"head": up}
        )

    def a_far_down(g):
        part = pl.ds(half, half)
        return remote(
            abuf.at[2, heads_of(g), part], abuf.at[3, heads_of(g), part], 8 + 9 * groups + g, {"head": down}
        )

    v_first.start()

    @pl.when(even)
    def _():
        v_direct.start()

    w_rel_up.start()
    w_rel_down.start()
    w_up.start()
    w_down.start()
    w_own.start()
    for copy in loads:
        copy.wait()

    near = jnp.where(s >= 1, 0.0, ABSENT).astype(F32)
    beyond = jnp.where(s >= 2, 0.0, ABSENT).astype(F32)

    def local(b):
        span = range(b * BATCH, (b + 1) * BATCH)
        done = local_heads(
            [q[:, lanes[x]] for x in span],
            [k[:, lanes[x]] for x in span],
            [w[:, lanes[x]] for x in span],
            [2.0 * jax.nn.sigmoid(beta[x : x + 1, :]) for x in span],
        )
        for x, (kt, qt, pb, _) in zip(span, done):
            kbuf[0, x] = kt
            qh, ql = halves(qt)
            qbuf[0, x] = qh
            qn[x, :, :SUB] = qh
            qn[x, :, SUB:] = ql
            ph, plow = halves(pb)
            pbuf[x, :, :SUB] = ph
            pbuf[x, :, SUB:] = plow
        return [d[3] for d in done]

    def with_ones(vals):
        return jnp.concatenate([vals, jnp.ones_like(vals)], 1)

    def own_share(b, scores):
        for x, parts in zip(range(b * BATCH, (b + 1) * BATCH), scores):
            for r, sc in enumerate(parts):
                rows = pl.ds(r * SUB, SUB)
                top = jnp.max(sc, 1, keepdims=True)
                e = jnp.exp2(sc - top).astype(BF16)
                both = dot1(e, with_ones(v[: (r + 1) * SUB, lanes[x]]))
                mst[x, rows] = wide(top)
                oacc[x, rows] = both[:, :SUB]
                lst[x, rows] = both[:, SUB:]

    def through_block(x, rows):
        pp = jnp.concatenate([pbuf[x, :, :SUB], pbuf[x, :, SUB:]], 0)
        return dot1(jnp.concatenate([rows, rows], 1), pp)

    def pass_on(g):
        k_first(g).wait_recv()
        for x in range(g * GROUP, (g + 1) * GROUP):
            kk = kbuf[1, x]
            kmid[x] = dot1(jnp.concatenate([kk, kk], 1), pbuf[x], NT).astype(BF16)
        k_second(g).start()
        q_first(g).wait_recv()
        for x in range(g * GROUP, (g + 1) * GROUP):
            qmid[x] = through_block(x, qbuf[1, x]).astype(BF16)
        q_second(g).start()

    def window(x):
        keys = jnp.concatenate([kbuf[1, x], kbuf[2, x]], 0)
        vals = jnp.concatenate([vbuf[0, :, lanes[x]], vbuf[1, :, lanes[x]]], 0)
        return jnp.concatenate([keys, keys], 1), with_ones(vals)

    def far_share(g):
        k_second(g).wait_recv()
        q_second(g).wait_recv()
        for x in range(g * GROUP, (g + 1) * GROUP):
            moved = jnp.concatenate(halves(through_block(x, qbuf[2, x])), 1)
            keys, vals = window(x)
            scores = dot1(moved, keys, NT)
            tops, weights = [], []
            for r in range(runs):
                sc = scores[r * SUB : (r + 1) * SUB]
                m0 = jnp.max(sc[:, :length], 1, keepdims=True)
                m1 = jnp.max(sc[:, length:], 1, keepdims=True)
                top = jnp.maximum(m0 + near, m1 + beyond)
                s0, s1 = jnp.maximum(top - near, m0), jnp.maximum(top - beyond, m1)
                tops.append(top)
                weights.append(
                    jnp.exp2(jnp.concatenate([sc[:, :length] - s0, sc[:, length:] - s1], 1)).astype(BF16)
                )
            both = dot1(jnp.concatenate(weights, 0), vals)
            for r in range(runs):
                rows = slice(r * SUB, (r + 1) * SUB)
                total = both[rows, SUB:]
                osend[x, rows] = (both[rows, :SUB] / total).astype(BF16)
                level = wide(tops[r]) + jnp.log2(total)
                lsend[x, r : r + 1] = jnp.sum(jnp.where(eye, level, 0.0), 0, keepdims=True)
        o_back(g).start()
        l_back(g).start()

    def near_share(g):
        for x in range(g * GROUP, (g + 1) * GROUP):
            keys, vals = window(x)
            scores = dot1(qn[x], keys, NT)
            keeps, weights = [], []
            for r in range(runs):
                rows = slice(r * SUB, (r + 1) * SUB)
                sc = scores[rows]
                m0 = jnp.max(sc[:, :length], 1, keepdims=True) + near
                m1 = jnp.max(sc[:, length:], 1, keepdims=True) + beyond
                before = mst[x, rows]
                top = jnp.maximum(before, wide(jnp.maximum(m0, m1)))
                shift = jnp.concatenate([top - near] * runs + [top - beyond] * runs, 1)
                weights.append(jnp.exp2(sc - shift).astype(BF16))
                keeps.append(jnp.exp2(before - top))
                mst[x, rows] = top
            both = dot1(jnp.concatenate(weights, 0), vals)
            for r in range(runs):
                rows = slice(r * SUB, (r + 1) * SUB)
                oacc[x, rows] = oacc[x, rows] * keeps[r] + both[rows, :SUB]
                lst[x, rows] = lst[x, rows] * keeps[r] + both[rows, SUB:]

    def merge(g):
        o_back(g).wait_recv()
        l_back(g).wait_recv()
        for x in range(g * GROUP, (g + 1) * GROUP):
            for r in range(runs):
                rows = pl.ds(r * SUB, SUB)
                level = jnp.where(s >= 3, lfar[x, r : r + 1], ABSENT)
                level = wide(jnp.sum(jnp.where(eye, level, 0.0), 1, keepdims=True))
                before = mst[x, rows]
                top = jnp.maximum(before, level)
                keep, other = jnp.exp2(before - top), jnp.exp2(level - top)
                total = lst[x, rows] * keep + other
                mix = oacc[x, rows] * keep + ofar[x, rows].astype(F32) * other
                abuf[0, x, rows] = (mix / total).astype(BF16)
        a_up(g).start()
        a_down(g).start()

    def gather_on(g):
        a_up(g).wait_recv()
        a_far_up(g).start()
        a_down(g).wait_recv()
        a_far_down(g).start()

    own_slot, up_slot, down_slot, far_slot = (0, 3), (1, 0), (2, 1), (3, 2)

    def project(*terms):
        left = [abuf[slot[0], x] for slot, g in terms for x in range(g * GROUP, (g + 1) * GROUP)]
        right = [
            wbuf[slot[1], x * SUB : (x + 1) * SUB] for slot, g in terms for x in range(g * GROUP, (g + 1) * GROUP)
        ]
        return dot1(jnp.concatenate(left, 1), jnp.concatenate(right, 0))

    def set_out(*which):
        for g in which:
            k_first(g).start()
            q_first(g).start()

    scores = local(0)
    set_out(0, 1)
    scores_late = local(1)
    set_out(2, 3)
    v_first.wait_recv()

    @pl.when(even)
    def _():
        v_passed.start()

    w_rel_up.wait_recv()
    w_far_up.start()
    w_rel_down.wait_recv()
    w_far_down.start()
    pass_on(0)
    pass_on(1)
    own_share(0, scores)
    own_share(1, scores_late)
    pass_on(2)
    pass_on(3)
    v_passed.wait_recv()
    last = groups - 1
    far_share(0)
    near_share(0)
    far_share(1)
    near_share(1)
    far_share(2)
    merge(0)
    near_share(2)
    far_share(3)
    merge(1)
    gather_on(0)
    for i, copy in enumerate((w_up, w_down)):
        copy.wait_recv()
        w_twin[i].start()
    w_far_up.wait_recv()
    w_far_down.wait_recv()
    w_twin[2].start()
    near_share(3)
    merge(2)
    gather_on(1)
    merge(3)
    gather_on(2)
    for copy in w_twin:
        copy.wait_recv()
    w_own.wait()
    every = range(groups)
    acc[...] = project(*((own_slot, g) for g in every))
    gather_on(last)
    acc[...] += project(*((slot, g) for slot in (up_slot, down_slot) for g in every))
    for g in every:
        a_far_up(g).wait_recv()
        a_far_down(g).wait_recv()
    out[...] = (acc[...] + project(*((far_slot, g) for g in every))).astype(BF16)

    for copy in (v_first, w_up, w_down, w_rel_up, w_rel_down, w_far_up, w_far_down, *w_twin):
        copy.wait_send()

    @pl.when(even)
    def _():
        v_direct.wait_send()
        v_passed.wait_send()

    for g in range(groups):
        for copy in (k_first, k_second, q_first, q_second, o_back, l_back, a_up, a_down, a_far_up, a_far_down):
            copy(g).wait_send()


def per_device(q, k, v, w, beta, wt):
    length, width = q.shape
    heads = width // SUB
    stat = pltpu.VMEM((heads, length, SUB), F32)
    rows = pltpu.VMEM((heads, length, SUB), BF16)

    def rows_of(count):
        return pltpu.VMEM((count, heads, length, SUB), BF16)

    scratch = [
        *[pltpu.VMEM((length, width), BF16)] * 4,
        rows_of(3), rows, rows_of(3), rows,
        pltpu.VMEM((2, length, width), BF16),
        pltpu.VMEM((heads, SUB, 2 * SUB), BF16),
        pltpu.VMEM((heads, length, 2 * SUB), BF16),
        stat, stat, stat, rows, rows,
        pltpu.VMEM((heads, 8, SUB), F32),
        pltpu.VMEM((heads, 8, SUB), F32),
        rows_of(4),
        pltpu.VMEM((4, width, width), BF16),
        pltpu.VMEM((2, width // 4, width), BF16),
        pltpu.VMEM((length, width), F32),
        pltpu.SemaphoreType.DMA((12 + 10 * heads // GROUP,)),
        pltpu.SemaphoreType.DMA((12 + 10 * heads // GROUP,)),
        pltpu.SemaphoreType.DMA((5,)),
    ]
    vmem, hbm = pl.BlockSpec(memory_space=pltpu.VMEM), pl.BlockSpec(memory_space=pl.ANY)
    return pl.pallas_call(
        kernel,
        out_shape=jax.ShapeDtypeStruct((length, width), BF16),
        in_specs=[hbm] * 4 + [vmem, hbm],
        out_specs=vmem,
        scratch_shapes=scratch,
        compiler_params=pltpu.CompilerParams(
            collective_id=0, has_side_effects=True, vmem_limit_bytes=56 << 20
        ),
    )(q, k, v, w, beta, wt)


def solution(mesh):
    return jax.shard_map(
        per_device,
        mesh=mesh,
        in_specs=(P("seq", "head"),) * 4 + (P("head", "seq"), P("head", None)),
        out_specs=P("seq", "head"),
        check_vma=False,
    )
```
